32 devices in a mesh: groups: 2 (over y), seq: 16 (over z, x, core).
Axes of the slice: x: 2, y: 2, z: 4, core: 2. Of those that a mesh axis runs over, the one named last changes fastest.
Arguments:
- queries: bfloat16 [8192, 2048], P(('groups', 'seq')), parts along dimension 0, may hold values from -128 to 128
- keys: bfloat16 [32768, 1024], P(('groups', 'seq')), parts along dimension 0, may hold values from -6 to 6
- values: bfloat16 [32768, 1024], P(('groups', 'seq')), parts along dimension 0, may hold values from -6 to 6
- dirty: int32 [32], P(('groups', 'seq')), parts along dimension 0, may hold values from -1 to 3
- spans: int32 [32, 2], P(('groups', 'seq')), parts along dimension 0, may hold values from 0 to 16384, as said below
Outputs:
- attended: bfloat16 [8192, 2048], P(('groups', 'seq')), parts along dimension 0
The draws below stay inside these ranges and needn't reach their ends.
There are 2 independent parts, one for each index of `groups`. The reference program is written for one: setup_inputs(seed, part) draws one part's arguments, and reference() takes and returns one part's arrays. A program takes and returns all parts, laid end to end along the dimension named above; each array names one. Nothing has to cross between parts.
Inputs may be any that keep to these rules, and one draw needn't show every extreme that they name: -1 marks a shard with no dirty block. `spans`: row k holds the start and the exclusive end of the one tombstoned span of shard k: k * 1024 <= start < end <= (k + 1) * 1024, with end - start from 1 to 32; the last shard's span has exactly 32 rows.
All inputs are finite; a program needn't handle non-finite values.
Results may differ from the reference program's by a relative error of at most 0.014.
Values may be sent and summed in bfloat16 or wider, within the bound.
A program may use at most 128 MiB of HBM per device.

```python
import math
import jax
import jax.numpy as jnp
from jax import lax

QUERY_HEADS = 16
KEY_VALUE_HEADS = 8
HEAD_DIMENSION = 128
WINDOW = 4096
BLOCK_ROWS = 256
SPAN = 32
SHARD_TOKENS = 1024
DOCUMENT_LENGTH = 16384
BLK_DEV = 4
SHARDS_BACK = 5
N_SEQ = 16


def draw_spans(key, part):
    count = N_SEQ
    index = jnp.arange(count, dtype=jnp.int32)
    lowest = max(SPAN // 3, 1)
    limit = jnp.maximum(1, lowest + (SPAN - lowest) * index // max(count - 1, 1))
    key_len, key_off = jax.random.split(jax.random.fold_in(key, 11))
    length = jax.random.randint(key_len, (count,), 1, limit + 1)
    length = jnp.where(index == count - 1, SPAN, length)
    offset = jax.random.randint(key_off, (count,), 0, SHARD_TOKENS - length + 1)
    start = index * SHARD_TOKENS + offset
    return jnp.stack([start, start + length], axis=1).astype(jnp.int32)


def draw_queries(key, part):
    count = N_SEQ * BLOCK_ROWS
    key_base, key_pick = jax.random.split(jax.random.fold_in(key, 23), 2)
    pick = jax.random.randint(key_pick, (count, 1), 0, 8)
    base = jnp.clip(jax.random.normal(key_base, (count, QUERY_HEADS * HEAD_DIMENSION), jnp.float32), -4.0, 4.0)
    factor = jnp.where(pick == 0, jnp.float32(32.0), jnp.float32(1.0))
    return (base * factor).astype(jnp.bfloat16)


def set_ends(array, own_key, smallest, high):
    extent = array.shape
    spot = [jax.random.randint(jax.random.fold_in(own_key, axis), (), 0, extent[axis]) for axis in range(len(extent))]
    array = array.at[tuple(spot)].set(smallest)
    longest = extent.index(max(extent))
    spot[longest] = (spot[longest] + 1) % extent[longest]
    return array.at[tuple(spot)].set(high)


def steps_of(rng, extent, pieces, low, top_value):
    level, own = 1.0, jax.random.fold_in(rng, 6)
    for axis_at, blocks in pieces:
        heights = jnp.exp(jax.random.uniform(jax.random.fold_in(own, axis_at), (blocks,), jnp.float32, low / len(pieces), top_value / len(pieces)))
        level = level * jnp.repeat(heights, extent[axis_at] // blocks).reshape([-1 if axis == axis_at else 1 for axis in range(len(extent))])
    return level


def normal_values(rng, shape, width, bound, pieces=(), held_as=jnp.bfloat16):
    entries = jax.random.normal(rng, shape, jnp.float32) * width
    if len(pieces) > 0:
        entries = steps_of(rng, shape, pieces, -0.22, 0.18) * entries
    return jnp.clip(entries, min=-bound, max=bound).astype(held_as)


def setup_inputs(seed: int = 0, part: int = 0) -> dict:
    key_list = jax.random.split(jax.random.key(seed), 6)
    own_keys = jax.random.split(jax.random.fold_in(key_list[5], part), 6)
    queries = draw_queries(jax.random.fold_in(jax.random.fold_in(key_list[5], part), 71), part)
    keys = normal_values(own_keys[1], (DOCUMENT_LENGTH, KEY_VALUE_HEADS * HEAD_DIMENSION), 1.0, 6.0, ((0, 16),))
    values = normal_values(own_keys[2], (DOCUMENT_LENGTH, KEY_VALUE_HEADS * HEAD_DIMENSION), 1.0, 6.0, ((0, 16),))
    dirty = set_ends(jax.random.randint(own_keys[3], (N_SEQ,), -1, BLK_DEV), jax.random.fold_in(own_keys[3], 1), -1, BLK_DEV - 1).astype(jnp.int32)
    spans = draw_spans(jax.random.fold_in(jax.random.fold_in(key_list[5], part), 71), part)
    return {"queries": queries, "keys": keys, "values": values, "dirty": dirty, "spans": spans}


softcap_limit = 50.0
query_scale = 144.0 ** -0.5


def locate(raw, spans):
    begin = spans[:, 0]
    finish = spans[:, 1]
    offset = raw[:, None] - begin[None, :]
    before = jnp.sum(jnp.clip(offset, 0, (finish - begin)[None, :]), axis=1)
    inside = jnp.sum(((raw[:, None] >= begin[None, :]) & (raw[:, None] < finish[None, :])).astype(jnp.int32), axis=1)
    return (raw - before).astype(jnp.int32), (inside == 0) & (raw >= 0)


def apply_rotary(field, place):
    half = field.shape[-1] // 2
    order = jnp.arange(half, dtype=jnp.float32)
    freq = jnp.exp(order * (-2.0 * math.log(10000.0) / field.shape[-1]))
    angle = place[:, None] * freq[None, :]
    cosine = jnp.cos(angle)[:, None, :]
    sine = jnp.sin(angle)[:, None, :]
    first = field[..., :half]
    second = field[..., half:]
    return jnp.concatenate([first * cosine - second * sine, second * cosine + first * sine], axis=-1)


def reference(queries, keys, values, dirty, spans):
    head_group = QUERY_HEADS // KEY_VALUE_HEADS
    window_margin = SHARDS_BACK * SHARD_TOKENS
    window_width = window_margin + SHARD_TOKENS
    padded_keys = jnp.concatenate([jnp.zeros((window_margin, KEY_VALUE_HEADS * HEAD_DIMENSION), jnp.bfloat16), keys], axis=0)
    padded_values = jnp.concatenate([jnp.zeros((window_margin, KEY_VALUE_HEADS * HEAD_DIMENSION), jnp.bfloat16), values], axis=0)

    def one_shard(shard_index):
        block = dirty[shard_index]
        chosen = jnp.maximum(block, 0)
        q_raw = (shard_index * SHARD_TOKENS + chosen * BLOCK_ROWS + jnp.arange(BLOCK_ROWS)).astype(jnp.int32)
        q_pos, q_live = locate(q_raw, spans)
        q_rows = lax.dynamic_slice(queries, ((shard_index * BLOCK_ROWS).astype(jnp.int32), jnp.int32(0)), (BLOCK_ROWS, QUERY_HEADS * HEAD_DIMENSION))
        query_rotary = (apply_rotary(q_rows.astype(jnp.float32).reshape(BLOCK_ROWS, QUERY_HEADS, HEAD_DIMENSION), q_pos.astype(jnp.float32)) * query_scale).astype(jnp.bfloat16)
        query_rotary = lax.optimization_barrier(query_rotary).astype(jnp.float32).reshape(BLOCK_ROWS, KEY_VALUE_HEADS, head_group, HEAD_DIMENSION)
        k_raw = (shard_index * SHARD_TOKENS - window_margin + jnp.arange(window_width)).astype(jnp.int32)
        key_position, k_live = locate(k_raw, spans)
        key_row_block = lax.dynamic_slice(padded_keys, ((shard_index * SHARD_TOKENS).astype(jnp.int32), jnp.int32(0)), (window_width, KEY_VALUE_HEADS * HEAD_DIMENSION))
        value_row_block = lax.dynamic_slice(padded_values, ((shard_index * SHARD_TOKENS).astype(jnp.int32), jnp.int32(0)), (window_width, KEY_VALUE_HEADS * HEAD_DIMENSION))
        key_rotary = apply_rotary(key_row_block.astype(jnp.float32).reshape(window_width, KEY_VALUE_HEADS, HEAD_DIMENSION), key_position.astype(jnp.float32)).astype(jnp.bfloat16)
        key_rotary = lax.optimization_barrier(key_rotary).astype(jnp.float32)
        score = jnp.einsum('qhgd,khd->hgqk', query_rotary, key_rotary)
        capped = softcap_limit * jnp.tanh(score / softcap_limit)
        allowed = k_live[None, :] & (k_raw[None, :] <= q_raw[:, None]) & ((q_pos[:, None] - key_position[None, :]) < WINDOW)
        weight = jnp.where(allowed[None, None], jnp.exp(capped), jnp.float32(0.0))
        total = jnp.sum(weight, axis=-1)
        total = jnp.where(total > 0, total, jnp.float32(1.0))
        rounded_weight = lax.optimization_barrier(weight.astype(jnp.bfloat16)).astype(jnp.float32)
        numerator = jnp.einsum('nexi,inv->xnev', rounded_weight, value_row_block.astype(jnp.float32).reshape(window_width, KEY_VALUE_HEADS, HEAD_DIMENSION))
        result = numerator / jnp.transpose(total, (2, 0, 1))[..., None]
        keep = q_live & (block >= 0)
        result = jnp.where(keep[:, None, None, None], result, jnp.float32(0.0))
        return result.reshape(BLOCK_ROWS, QUERY_HEADS * HEAD_DIMENSION).astype(jnp.bfloat16)

    blocks = lax.map(one_shard, jnp.arange(N_SEQ, dtype=jnp.int32))
    return blocks.reshape(N_SEQ * BLOCK_ROWS, QUERY_HEADS * HEAD_DIMENSION)
```

```python
import functools
import math

import jax
import jax.numpy as jnp
from jax import lax
from jax.experimental import pallas as pl
from jax.experimental.pallas import tpu as pltpu
from jax.sharding import PartitionSpec as P

HEAD = 128
WINDOW = 4096
BLOCK = 256
CAP = 50.0
QUERY_SCALE = 144.0 ** (-0.5)
LOG2E = math.log2(math.e)
VMEM = pl.BlockSpec(memory_space=pltpu.VMEM)
SMEM = pl.BlockSpec(memory_space=pltpu.SMEM)
PARAMS = pltpu.CompilerParams(vmem_limit_bytes=48 * 1024 * 1024)


def removed_before(meta, shard):
    def add(s, total):
        return total + meta[3 * s + 2] - meta[3 * s + 1]

    return lax.fori_loop(0, shard, add, jnp.int32(0))


def tables(row, base, begin, length):
    lane = lax.broadcasted_iota(jnp.int32, row.shape, 1)
    order = (lane % (HEAD // 2)).astype(jnp.float32)
    freq = jnp.exp(order * (-2.0 * math.log(10000.0) / HEAD))
    place = row - base - jnp.clip(row - begin, 0, length)
    angle = place.astype(jnp.float32) * freq
    low = lane < HEAD // 2
    cosine, sine = jnp.cos(angle), jnp.sin(angle)
    cosine_swap = pltpu.roll(cosine, HEAD // 2, 1)
    sine_swap = pltpu.roll(sine, HEAD // 2, 1)
    return (
        (jnp.where(low, cosine, cosine_swap), jnp.where(low, -sine, sine_swap)),
        (jnp.where(low, cosine_swap, cosine), jnp.where(low, -sine_swap, sine)),
    )


def rotate(x, table):
    x = x.astype(jnp.float32)
    return x * table[0] + pltpu.roll(x, HEAD // 2, 1) * table[1]


def rope_q_kernel(meta, mine, other, out):
    me = lax.axis_index("seq")
    core = me % 2
    rows_shard = 1024
    half = BLOCK // 2
    for which, ref in enumerate((mine, other)):
        slot = core if which == 0 else 1 - core
        shard = me - core + slot
        block = jnp.maximum(meta[3 * shard], 0)
        begin = meta[3 * shard + 1]
        length = meta[3 * shard + 2] - begin
        base = removed_before(meta, shard)
        raw0 = shard * rows_shard + block * BLOCK
        tile = 32

        @pl.loop(0, half // tile)
        def _(step):
            at = pl.multiple_of(step * tile, tile)
            row = lax.broadcasted_iota(jnp.int32, (tile, HEAD), 0) + raw0 + at
            lane = lax.broadcasted_iota(jnp.int32, (tile, HEAD), 1)
            row = row + jnp.where(lane < HEAD // 2, 0, half)
            both = tables(row, base, begin, length)
            for part in range(2):
                src = pl.multiple_of(at + part * half, tile)
                dst = pl.multiple_of(slot * BLOCK + src, tile)
                for h in range(out.shape[1] // HEAD):
                    cols = pl.ds(h * HEAD, HEAD)
                    x = rotate(ref[pl.ds(src, tile), cols], both[part]) * QUERY_SCALE
                    out[pl.ds(dst, tile), cols] = x.astype(jnp.bfloat16)


def prep_kv_kernel(meta, k_mine, k_other, v_mine, v_other, k_out, v_out, live_out):
    me = lax.axis_index("seq")
    core = me % 2
    rows = k_mine.shape[0]
    half = rows // 2
    for which, (k_ref, v_ref) in enumerate(((k_mine, v_mine), (k_other, v_other))):
        slot = core if which == 0 else 1 - core
        shard = me - core + slot
        begin = meta[3 * shard + 1]
        finish = meta[3 * shard + 2]
        base = removed_before(meta, shard)
        raw0 = shard * rows
        tile = 32

        @pl.loop(0, half // tile)
        def _(step):
            at = pl.multiple_of(step * tile, tile)
            iota = lax.broadcasted_iota(jnp.int32, (tile, HEAD), 0)
            lane = lax.broadcasted_iota(jnp.int32, (tile, HEAD), 1)
            row = iota + raw0 + at + jnp.where(lane < HEAD // 2, 0, half)
            both = tables(row, base, begin, finish - begin)
            for part in range(2):
                src = pl.multiple_of(at + part * half, tile)
                dst = pl.multiple_of(slot * rows + src, tile)
                raw = iota + raw0 + src
                live = jnp.where((raw >= begin) & (raw < finish), 0.0, 1.0)
                live_out[pl.ds(dst, tile), :] = live.astype(jnp.bfloat16)
                for h in range(k_out.shape[1] // HEAD):
                    cols = pl.ds(h * HEAD, HEAD)
                    x = rotate(k_ref[pl.ds(src, tile), cols], both[part])
                    k_out[pl.ds(dst, tile), cols] = x.astype(jnp.bfloat16)
                    y = v_ref[pl.ds(src, tile), cols].astype(jnp.float32) * live
                    v_out[pl.ds(dst, tile), cols] = y.astype(jnp.bfloat16)


def visit(meta, q_ref, k_ref, v_ref, live_ref, acc, at, slot, mask):
    kv_heads = k_ref.shape[1] // HEAD
    rows = pl.ds(pl.multiple_of(at, BLOCK), BLOCK)
    q_rows = pl.ds(pl.multiple_of(slot * BLOCK, BLOCK), BLOCK)

    def scores(h):
        q = jnp.concatenate(
            [q_ref[q_rows, pl.ds((2 * h + g) * HEAD, HEAD)] for g in range(2)], axis=0
        )
        k = k_ref[rows, pl.ds(h * HEAD, HEAD)]
        return lax.dot_general(
            q, k, (((1,), (1,)), ((), ())), preferred_element_type=jnp.float32
        )

    s = scores(0)
    for h in range(kv_heads):
        ahead = scores(h + 1) if h + 1 < kv_heads else None
        weight = jnp.exp2(jnp.tanh(s * (1.0 / CAP)) * (CAP * LOG2E))
        if mask is not None:
            weight = jnp.where(mask, weight, 0.0)
        v = jnp.concatenate([v_ref[rows, pl.ds(h * HEAD, HEAD)], live_ref[rows, :]], axis=1)
        acc[h] += jnp.dot(weight.astype(jnp.bfloat16), v, preferred_element_type=jnp.float32)
        s = ahead


def allowed(meta, shard_q, raw_q, shard_k, raw_k):
    column = lax.broadcasted_iota(jnp.int32, (2 * BLOCK, 1), 0)
    q = raw_q + jnp.where(column < BLOCK, column, column - BLOCK)
    k = raw_k + lax.broadcasted_iota(jnp.int32, (1, BLOCK), 1)
    begin_q, end_q = meta[3 * shard_q + 1], meta[3 * shard_q + 2]
    begin_k, end_k = meta[3 * shard_k + 1], meta[3 * shard_k + 2]
    between = removed_before(meta, shard_q) - removed_before(meta, shard_k)
    q_place = q - between - jnp.clip(q - begin_q, 0, end_q - begin_q)
    k_place = k - jnp.clip(k - begin_k, 0, end_k - begin_k)
    return (k <= q) & (q_place - k_place < WINDOW)


def attend_kernel(away, n, tail, meta, q_ref, k_ref, v_ref, live_ref, *rest):
    if tail:
        tail_k, tail_v, tail_live, out, acc = rest
    else:
        out, acc = rest
    me = lax.axis_index("seq")
    chip = me // 2
    rows = k_ref.shape[0] // 2
    per_shard = rows // BLOCK
    count = 2 * per_shard
    first = chip * count
    kv_heads = k_ref.shape[1] // HEAD
    reach = WINDOW // BLOCK

    @pl.loop(0, 2)
    def _(slot):
        wanted = 2 * (chip + away) + slot
        shard = jnp.minimum(wanted, n - 1)
        block = meta[3 * shard]
        on = (wanted < n) & (block >= 0)
        block = jnp.maximum(block, 0)
        g = shard * per_shard + block - first
        lo = jnp.clip(g - reach - 1, 0, count)
        full_lo = jnp.clip(g - reach + 1, 0, count)
        full_hi = jnp.clip(g, 0, count)
        hi = jnp.clip(g + 1, 0, count)
        raw_q = (first + g) * BLOCK
        acc[...] = jnp.zeros_like(acc)

        @pl.loop(full_lo, jnp.where(on, full_hi, full_lo))
        def _(j):
            visit(meta, q_ref, k_ref, v_ref, live_ref, acc, j * BLOCK, slot, None)

        front = full_lo - lo

        @pl.loop(0, jnp.where(on, front + hi - full_hi, 0))
        def _(i):
            j = jnp.where(i < front, lo + i, full_hi + i - front)
            shard_k = 2 * chip + j // per_shard
            mask = allowed(meta, shard, raw_q, shard_k, (first + j) * BLOCK)
            visit(meta, q_ref, k_ref, v_ref, live_ref, acc, j * BLOCK, slot, mask)

        if tail:
            raw_k = (first + g - reach - 1) * BLOCK

            @pl.when(on & (g == 0) & (raw_k >= 0))
            def _():
                shard_k = jnp.maximum((first + g - reach - 1) // per_shard, 0)
                mask = allowed(meta, shard, raw_q, shard_k, raw_k)
                visit(meta, q_ref, tail_k, tail_v, tail_live, acc, 0, slot, mask)

        to = pl.ds(pl.multiple_of(slot * BLOCK, BLOCK), BLOCK)
        lane = lax.broadcasted_iota(jnp.int32, (BLOCK, HEAD), 1)
        packed = jnp.zeros((BLOCK, HEAD), jnp.float32)
        for h in range(kv_heads):
            for part in range(2):
                head = 2 * h + part
                mine = pl.ds(part * BLOCK, BLOCK)
                out[to, pl.ds(head * HEAD, HEAD)] = acc[h, mine, pl.ds(0, HEAD)].astype(
                    jnp.bfloat16
                )
                total = acc[h, mine, pl.ds(HEAD, HEAD)]
                coarse = total.astype(jnp.bfloat16).astype(jnp.float32)
                packed = jnp.where(lane == head, coarse, packed)
                packed = jnp.where(lane == head + 2 * kv_heads, total - coarse, packed)
        out[to, pl.ds(2 * kv_heads * HEAD, HEAD)] = packed.astype(jnp.bfloat16)


def finish_kernel(meta, *refs):
    parts, out = refs[:-1], refs[-1]
    me = lax.axis_index("seq")
    heads = out.shape[1] // HEAD
    per = BLOCK

    @pl.loop(0, 2)
    def _(slot):
        shard = me - me % 2 + slot
        block = meta[3 * shard]
        begin, end = meta[3 * shard + 1], meta[3 * shard + 2]
        raw0 = shard * 1024 + jnp.maximum(block, 0) * BLOCK
        rows = pl.ds(pl.multiple_of(slot * per, per), per)
        raw = raw0 + lax.broadcasted_iota(jnp.int32, (per, HEAD), 0)
        gone = (raw >= begin) & (raw < end)
        keep = jnp.logical_not(gone) & (block >= 0)
        totals = jnp.zeros((per, HEAD), jnp.float32)
        for part in parts:
            totals += part[rows, pl.ds(heads * HEAD, HEAD)].astype(jnp.float32)
        for h in range(heads):
            cols = pl.ds(h * HEAD, HEAD)
            total = totals[:, h : h + 1] + totals[:, heads + h : heads + h + 1]
            total = jnp.broadcast_to(jnp.where(total > 0, total, 1.0), (per, HEAD))
            value = jnp.zeros((per, HEAD), jnp.float32)
            for part in parts:
                value += part[rows, cols].astype(jnp.float32)
            value = jnp.where(keep, value / total, 0.0)
            out[rows, cols] = value.astype(jnp.bfloat16)


def call(kernel, inputs, shapes, scratch=(), cost=None):
    return pl.pallas_call(
        kernel,
        out_shape=shapes,
        in_specs=[SMEM] + [VMEM] * (len(inputs) - 1),
        out_specs=jax.tree.map(lambda _: VMEM, shapes),
        scratch_shapes=list(scratch),
        compiler_params=PARAMS,
        cost_estimate=cost,
    )(*inputs)


def shift(array, by, n):
    pairs = [(i, i + by) for i in range(n) if 0 <= i + by < n]
    return lax.ppermute(array, "seq", pairs)


def flip(array, n):
    return lax.ppermute(array, "seq", [(i, i ^ 1) for i in range(n)])


def half_of(array, which):
    width = array.shape[1] // 2
    return lax.dynamic_slice_in_dim(array, which * width, width, axis=1)


def body(queries, keys, values, dirty, spans):
    n = lax.axis_size("seq")
    core = lax.axis_index("seq") % 2
    bf = jnp.bfloat16
    own = jnp.concatenate([dirty[:, None], spans], axis=1)
    meta = lax.all_gather(own, "seq", axis=0, tiled=True).reshape(-1)
    q_other = flip(half_of(queries, 1 - core), n)
    k_other = flip(half_of(keys, 1 - core), n)
    v_other = flip(half_of(values, 1 - core), n)
    q_mine, k_mine, v_mine = (half_of(a, core) for a in (queries, keys, values))
    rows, width = k_mine.shape
    q = call(
        rope_q_kernel,
        (meta, q_mine, q_other),
        jax.ShapeDtypeStruct((2 * BLOCK, q_mine.shape[1]), bf),
        cost=pl.CostEstimate(flops=10**7, bytes_accessed=2**21, transcendentals=0),
    )
    visitors = [shift(q, -2 * d, n) for d in (1, 2)]
    k, v, live = call(
        prep_kv_kernel,
        (meta, k_mine, k_other, v_mine, v_other),
        (
            jax.ShapeDtypeStruct((2 * rows, width), bf),
            jax.ShapeDtypeStruct((2 * rows, width), bf),
            jax.ShapeDtypeStruct((2 * rows, HEAD), bf),
        ),
        cost=pl.CostEstimate(flops=10**8, bytes_accessed=2**23, transcendentals=0),
    )
    last = jnp.concatenate([k[-BLOCK:], v[-BLOCK:], live[-BLOCK:]], axis=1)
    last = shift(last, 6, n)
    tail = (last[:, :width], last[:, width : 2 * width], last[:, 2 * width :])
    shape = jax.ShapeDtypeStruct((2 * BLOCK, q.shape[1] + HEAD), bf)
    scratch = [pltpu.VMEM((width // HEAD, 2 * BLOCK, 2 * HEAD), jnp.float32)]
    cost = pl.CostEstimate(flops=6 * 10**9, bytes_accessed=2**23, transcendentals=10**7)

    def attend(away, visitor, extra):
        kernel = functools.partial(attend_kernel, away, n, bool(extra))
        return call(kernel, (meta, visitor, k, v, live) + extra, shape, scratch, cost)

    back = [shift(attend(d, visitors[d - 1], ()), 2 * d, n) for d in (1, 2)]
    parts = (attend(0, q, tail), *back)
    done = call(finish_kernel, (meta,) + parts, jax.ShapeDtypeStruct(q.shape, bf))
    mine = lax.dynamic_slice_in_dim(done, core * BLOCK, BLOCK, axis=0)
    other = flip(lax.dynamic_slice_in_dim(done, (1 - core) * BLOCK, BLOCK, axis=0), n)
    return jnp.where(
        core == 0,
        jnp.concatenate([mine, other], axis=1),
        jnp.concatenate([other, mine], axis=1),
    )


def solution(mesh):
    placed = (
        P(("groups", "seq"), None),
        P(("groups", "seq"), None),
        P(("groups", "seq"), None),
        P(("groups", "seq")),
        P(("groups", "seq"), None),
    )
    return jax.shard_map(
        body, mesh=mesh, in_specs=placed, out_specs=P(("groups", "seq"), None), check_vma=False
    )
```

```python
import functools
import math

import jax
import jax.numpy as jnp
from jax import lax
from jax.experimental import pallas as pl
from jax.experimental.pallas import tpu as pltpu
from jax.sharding import PartitionSpec as P

HEAD = 128
WINDOW = 4096
BLOCK = 256
CAP = 50.0
QUERY_SCALE = 144.0 ** (-0.5)
LOG2E = math.log2(math.e)
VMEM = pl.BlockSpec(memory_space=pltpu.VMEM)
ANY = pl.BlockSpec(memory_space=pl.ANY)
SMEM = pl.BlockSpec(memory_space=pltpu.SMEM)
MESH = pl.DeviceIdType.MESH


def removed_before(meta, shard):
    def add(s, total):
        return total + meta[3 * s + 2] - meta[3 * s + 1]

    return lax.fori_loop(0, shard, add, jnp.int32(0))


def tables(row, base, begin, length):
    lane = lax.broadcasted_iota(jnp.int32, row.shape, 1)
    order = (lane % (HEAD // 2)).astype(jnp.float32)
    freq = jnp.exp(order * (-2.0 * math.log(10000.0) / HEAD))
    place = row - base - jnp.clip(row - begin, 0, length)
    angle = place.astype(jnp.float32) * freq
    low = lane < HEAD // 2
    cosine, sine = jnp.cos(angle), jnp.sin(angle)
    cosine_swap = pltpu.roll(cosine, HEAD // 2, 1)
    sine_swap = pltpu.roll(sine, HEAD // 2, 1)
    return (
        (jnp.where(low, cosine, cosine_swap), jnp.where(low, -sine, sine_swap)),
        (jnp.where(low, cosine_swap, cosine), jnp.where(low, -sine_swap, sine)),
    )


def rotate(x, table):
    x = x.astype(jnp.float32)
    return x * table[0] + pltpu.roll(x, HEAD // 2, 1) * table[1]


def at_seq(device):
    return {"seq": device}


def greet(conditions_devices):
    barrier = pltpu.get_barrier_semaphore()
    count = jnp.int32(0)
    for condition, device in conditions_devices:

        @pl.when(condition)
        def _():
            pl.semaphore_signal(barrier, inc=1, device_id=at_seq(device), device_id_type=MESH)

        count = count + jnp.where(condition, 1, 0)
    pl.semaphore_wait(barrier, count)


def exchange_kernel(n, own, q, k, v, meta, q_all, k_all, v_all, meta_sems, sems, local_sems):
    me = lax.axis_index("seq")
    core = lax.rem(me, 2)
    peer = me + 1 - 2 * core
    barrier = pltpu.get_barrier_semaphore()

    @pl.loop(1, n)
    def _(i):
        target = lax.rem(me + i, n)
        pl.semaphore_signal(barrier, inc=1, device_id=at_seq(target), device_id_type=MESH)

    pl.semaphore_wait(barrier, n - 1)

    def meta_copy(i, owner, target):
        return pltpu.make_async_remote_copy(
            src_ref=own,
            dst_ref=meta.at[owner],
            send_sem=meta_sems.at[0, i],
            recv_sem=meta_sems.at[1, owner],
            device_id=at_seq(target),
            device_id_type=MESH,
        )

    @pl.loop(1, n)
    def _(i):
        meta_copy(i, me, lax.rem(me + i, n)).start()

    copies = []
    for index, (source, target) in enumerate(((q, q_all), (k, k_all), (v, v_all))):
        rows, width = source.shape[0], source.shape[1] // 2
        theirs = pl.ds(pl.multiple_of((1 - core) * width, HEAD), width)
        mine = pl.ds(pl.multiple_of(core * width, HEAD), width)
        to = pl.ds(pl.multiple_of(core * rows, BLOCK), rows)
        remote = pltpu.make_async_remote_copy(
            src_ref=source.at[:, theirs],
            dst_ref=target.at[to, :],
            send_sem=sems.at[0, index],
            recv_sem=sems.at[1, index],
            device_id=at_seq(peer),
            device_id_type=MESH,
        )
        remote.start()
        local = pltpu.make_async_copy(source.at[:, mine], target.at[to, :], local_sems.at[index])
        local.start()
        copies += [remote, local]
    local = pltpu.make_async_copy(own, meta.at[me], local_sems.at[3])
    local.start()
    for copy in copies + [local]:
        copy.wait()

    @pl.loop(1, n)
    def _(i):
        meta_copy(i, me, lax.rem(me + i, n)).wait_send()
        sender = lax.rem(me + n - i, n)
        meta_copy(i, sender, sender).wait_recv()


def rope_q(meta, shard, slot, raw_rows, source, out):
    half = BLOCK // 2
    block = jnp.maximum(meta[3 * shard], 0)
    begin = meta[3 * shard + 1]
    length = meta[3 * shard + 2] - begin
    base = removed_before(meta, shard)
    raw0 = shard * raw_rows + block * BLOCK
    tile = 32

    @pl.loop(0, half // tile)
    def _(step):
        at = step * tile
        row = lax.broadcasted_iota(jnp.int32, (tile, HEAD), 0) + raw0 + at
        lane = lax.broadcasted_iota(jnp.int32, (tile, HEAD), 1)
        row = row + jnp.where(lane < HEAD // 2, 0, half)
        both = tables(row, base, begin, length)
        for part in range(2):
            rows = pl.ds(pl.multiple_of(slot * BLOCK + at + part * half, tile), tile)
            here = pl.ds(pl.multiple_of(at + part * half, tile), tile)
            for h in range(out.shape[1] // HEAD):
                cols = pl.ds(h * HEAD, HEAD)
                x = rotate(source[rows, cols], both[part]) * QUERY_SCALE
                out[here, cols] = x.astype(jnp.bfloat16)


def prepare(meta, shard, slot, k_ref, v_ref, k_out, v_out, live_out):
    rows = k_ref.shape[0] // 2
    half = rows // 2
    begin = meta[3 * shard + 1]
    finish = meta[3 * shard + 2]
    base = removed_before(meta, shard)
    raw0 = shard * rows
    tile = 32

    @pl.loop(0, half // tile)
    def _(step):
        at = step * tile
        iota = lax.broadcasted_iota(jnp.int32, (tile, HEAD), 0)
        lane = lax.broadcasted_iota(jnp.int32, (tile, HEAD), 1)
        row = iota + raw0 + at + jnp.where(lane < HEAD // 2, 0, half)
        both = tables(row, base, begin, finish - begin)
        for part in range(2):
            src = at + part * half
            place = pl.ds(pl.multiple_of(slot * rows + src, tile), tile)
            raw = iota + raw0 + src
            live = jnp.where((raw >= begin) & (raw < finish), 0.0, 1.0)
            live_out[place, :] = live.astype(jnp.bfloat16)
            for h in range(k_out.shape[1] // HEAD):
                cols = pl.ds(h * HEAD, HEAD)
                x = rotate(k_ref[place, cols], both[part])
                k_out[place, cols] = x.astype(jnp.bfloat16)
                y = v_ref[place, cols].astype(jnp.float32) * live
                v_out[place, cols] = y.astype(jnp.bfloat16)


def visit(q_ref, k_ref, v_ref, live_ref, acc, at, size, mask):
    kv_heads = k_ref.shape[1] // HEAD
    rows = pl.ds(at if isinstance(at, int) else pl.multiple_of(at, BLOCK), size)

    def scores(h):
        q = jnp.concatenate(
            [q_ref[:, pl.ds((2 * h + g) * HEAD, HEAD)] for g in range(2)], axis=0
        )
        k = k_ref[rows, pl.ds(h * HEAD, HEAD)]
        return lax.dot_general(
            q, k, (((1,), (1,)), ((), ())), preferred_element_type=jnp.float32
        )

    s = scores(0)
    for h in range(kv_heads):
        ahead = scores(h + 1) if h + 1 < kv_heads else None
        weight = jnp.exp2(jnp.tanh(s * (1.0 / CAP)) * (CAP * LOG2E))
        if mask is not None:
            weight = jnp.where(mask, weight, 0.0)
        v = jnp.concatenate([v_ref[rows, pl.ds(h * HEAD, HEAD)], live_ref[rows, :]], axis=1)
        acc[h] += jnp.dot(weight.astype(jnp.bfloat16), v, preferred_element_type=jnp.float32)
        s = ahead


def allowed(meta, n, shard_q, shard_k, raw_rows, at_k, size):
    shard_q = jnp.clip(shard_q, 0, n - 1)
    shard_k = jnp.clip(shard_k, 0, n - 1)
    column = lax.broadcasted_iota(jnp.int32, (2 * BLOCK, 1), 0)
    raw_q = shard_q * raw_rows + jnp.maximum(meta[3 * shard_q], 0) * BLOCK
    q = raw_q + jnp.where(column < BLOCK, column, column - BLOCK)
    k = shard_k * raw_rows + at_k + lax.broadcasted_iota(jnp.int32, (1, size), 1)
    begin_q, end_q = meta[3 * shard_q + 1], meta[3 * shard_q + 2]
    begin_k, end_k = meta[3 * shard_k + 1], meta[3 * shard_k + 2]
    between = removed_before(meta, shard_q) - removed_before(meta, shard_k)
    q_place = q - between - jnp.clip(q - begin_q, 0, end_q - begin_q)
    k_place = k - jnp.clip(k - begin_k, 0, end_k - begin_k)
    return (k <= q) & (q_place - k_place < WINDOW)


def pack(acc, out):
    kv_heads = acc.shape[0]
    lane = lax.broadcasted_iota(jnp.int32, (BLOCK, HEAD), 1)
    packed = jnp.zeros((BLOCK, HEAD), jnp.float32)
    for h in range(kv_heads):
        for part in range(2):
            head = 2 * h + part
            mine = pl.ds(part * BLOCK, BLOCK)
            out[:, pl.ds(head * HEAD, HEAD)] = acc[h, mine, pl.ds(0, HEAD)].astype(jnp.bfloat16)
            total = acc[h, mine, pl.ds(HEAD, HEAD)]
            coarse = total.astype(jnp.bfloat16).astype(jnp.float32)
            packed = jnp.where(lane == head, coarse, packed)
            packed = jnp.where(lane == head + 2 * kv_heads, total - coarse, packed)
    out[:, pl.ds(2 * kv_heads * HEAD, HEAD)] = packed.astype(jnp.bfloat16)


def finish(meta, shard, raw_rows, parts, out):
    heads = out.shape[1] // HEAD
    block = meta[3 * shard]
    begin, end = meta[3 * shard + 1], meta[3 * shard + 2]
    raw0 = shard * raw_rows + jnp.maximum(block, 0) * BLOCK
    tile = 64

    @pl.loop(0, BLOCK // tile)
    def _(step):
        here = pl.ds(pl.multiple_of(step * tile, tile), tile)
        raw = raw0 + step * tile + lax.broadcasted_iota(jnp.int32, (tile, HEAD), 0)
        keep = ((raw < begin) | (raw >= end)) & (block >= 0)
        totals = jnp.zeros((tile, HEAD), jnp.float32)
        for part in parts:
            totals += part[here, pl.ds(heads * HEAD, HEAD)].astype(jnp.float32)
        for h in range(heads):
            cols = pl.ds(h * HEAD, HEAD)
            total = totals[:, h : h + 1] + totals[:, heads + h : heads + h + 1]
            total = jnp.broadcast_to(jnp.where(total > 0, total, 1.0), (tile, HEAD))
            value = jnp.zeros((tile, HEAD), jnp.float32)
            for part in parts:
                value += part[here, cols].astype(jnp.float32)
            out[here, cols] = jnp.where(keep, value / total, 0.0).astype(jnp.bfloat16)


def serve_kernel(
    n, reach, meta, q_raw, k_raw, v_raw, out,
    q, k, v, live, q_in, part_out, part_in, own, tail_k, tail_v, tail_live, acc, done, give_away, got,
    q_sems, part_sems, tail_sems, done_sems,
):
    me = lax.axis_index("seq")
    core = lax.rem(me, 2)
    chip = lax.div(me, 2)
    chips = n // 2
    peer = me + 1 - 2 * core
    rows = k.shape[0] // 2
    per = rows // BLOCK
    far = reach + 1
    wide = 2 * BLOCK
    first = 2 * chip
    greet(
        [(me >= 0, peer)]
        + [(chip >= d, me - 2 * d) for d in range(1, far + 1)]
        + [(chip + d < chips, me + 2 * d) for d in range(1, far + 1)]
    )

    def q_copy(d, slot):
        return pltpu.make_async_remote_copy(
            src_ref=q[slot],
            dst_ref=q_in[2 * d - 2 + slot],
            send_sem=q_sems.at[0, d - 1, slot],
            recv_sem=q_sems.at[1, d - 1, slot],
            device_id=at_seq(jnp.maximum(me - 2 * d, core)),
            device_id_type=MESH,
        )

    def part_copy(d, slot):
        return pltpu.make_async_remote_copy(
            src_ref=part_out[2 * d - 2 + slot],
            dst_ref=part_in[2 * d - 2 + slot],
            send_sem=part_sems.at[0, d - 1, slot],
            recv_sem=part_sems.at[1, d - 1, slot],
            device_id=at_seq(jnp.minimum(me + 2 * d, n - 2 + core)),
            device_id_type=MESH,
        )

    last = pl.ds(2 * rows - BLOCK, BLOCK)
    tails = [
        pltpu.make_async_remote_copy(
            src_ref=source.at[last, :],
            dst_ref=target,
            send_sem=tail_sems.at[0, i],
            recv_sem=tail_sems.at[1, i],
            device_id=at_seq(jnp.minimum(me + 2 * far, n - 2 + core)),
            device_id_type=MESH,
        )
        for i, (source, target) in enumerate(((k, tail_k), (v, tail_v), (live, tail_live)))
    ]

    for slot in range(2):
        rope_q(meta, first + slot, slot, rows, q_raw, q[slot])
    for slot in range(2):
        for d in range(1, reach + 1):

            @pl.when(chip >= d)
            def _():
                q_copy(d, slot).start()

    for d in range(1, reach + 1):

        @pl.when(chip < d)
        def _():
            for ref in part_in[2 * d - 2 : 2 * d]:
                ref[...] = jnp.zeros_like(ref)

    @pl.loop(0, 2)
    def _(i):
        slot = 1 - i
        prepare(meta, first + slot, slot, k_raw, v_raw, k, v, live)

    @pl.when(chip + far < chips)
    def _():
        for copy in tails:
            copy.start()

    def masked(source, shard_q, j, size):
        shard_k = first + lax.div(j, per)
        mask = allowed(meta, n, shard_q, shard_k, rows, lax.rem(j, per) * BLOCK, size)
        visit(source, k, v, live, acc, j * BLOCK, size, mask)

    def plain(source, j):
        visit(source, k, v, live, acc, j * BLOCK, wide, None)

    def own_part(slot):
        acc[...] = jnp.zeros_like(acc)
        if slot == 1:

            @pl.loop(0, per // 2)
            def _(i):
                plain(q[slot], 2 * i)

        @pl.loop(0, per // 2)
        def _(i):
            masked(q[slot], first + slot, slot * per + 2 * i, wide)

    own_part(1)
    pack(acc, own[1])

    for d in range(1, reach + 1):

        @pl.when(chip + d < chips)
        def _():
            for slot in range(2):
                source = q_in[2 * d - 2 + slot]
                q_copy(d, slot).wait_recv()
                acc[...] = jnp.zeros_like(acc)
                if d < reach:

                    @pl.loop(0, per)
                    def _(i):
                        plain(source, 2 * i)

                else:
                    shard_q = first + 2 * d + slot

                    @pl.loop(0, per // 2)
                    def _(i):
                        masked(source, shard_q, slot * per + 2 * i, wide)

                    if slot == 0:

                        @pl.loop(0, per // 2)
                        def _(i):
                            plain(source, per + 2 * i)

                    else:
                        masked(source, shard_q, jnp.int32(per - 1), BLOCK)

                pack(acc, part_out[2 * d - 2 + slot])
                part_copy(d, slot).start()

    own_part(0)

    @pl.when(chip >= far)
    def _():
        for copy in tails:
            copy.wait_recv()
        mask = allowed(meta, n, first, first - 2 * far + 1, rows, rows - BLOCK, BLOCK)
        visit(q[0], tail_k, tail_v, tail_live, acc, 0, BLOCK, mask)

    pack(acc, own[0])
    for d in range(1, reach + 1):

        @pl.when(chip >= d)
        def _():
            for slot in range(2):
                part_copy(d, slot).wait_recv()

    def final(slot, out):
        finish(meta, first + slot, rows, [own[slot]] + list(part_in[slot::2]), out)

    for slot in range(2):

        @pl.when(core == slot)
        def _():
            final(1 - slot, give_away)

    give = pltpu.make_async_remote_copy(
        src_ref=give_away,
        dst_ref=got,
        send_sem=done_sems.at[0],
        recv_sem=done_sems.at[1],
        device_id=at_seq(peer),
        device_id_type=MESH,
    )
    give.start()
    for slot in range(2):

        @pl.when(core == slot)
        def _():
            final(slot, done)

    width = done.shape[1]
    out[:, pl.ds(pl.multiple_of(core * width, HEAD), width)] = done[...]
    give.wait()
    out[:, pl.ds(pl.multiple_of((1 - core) * width, HEAD), width)] = got[...]

    for d in range(1, reach + 1):

        @pl.when(chip >= d)
        def _():
            for slot in range(2):
                q_copy(d, slot).wait_send()

        @pl.when(chip + d < chips)
        def _():
            for slot in range(2):
                part_copy(d, slot).wait_send()

    @pl.when(chip + far < chips)
    def _():
        for copy in tails:
            copy.wait_send()


def body(queries, keys, values, dirty, spans):
    n = lax.axis_size("seq")
    bf = jnp.bfloat16
    shape = jax.ShapeDtypeStruct
    rows, width = keys.shape[0], keys.shape[1] // 2
    q_width = queries.shape[1] // 2
    reach = WINDOW // (2 * rows)
    own = jnp.concatenate([dirty[:, None], spans], axis=1)
    own = jnp.pad(own, ((0, 7), (0, HEAD - 3)))
    meta, q, k, v = pl.pallas_call(
        functools.partial(exchange_kernel, n),
        out_shape=(
            shape((n, 8, HEAD), jnp.int32),
            shape((2 * BLOCK, q_width), bf),
            shape((2 * rows, width), bf),
            shape((2 * rows, width), bf),
        ),
        in_specs=[ANY] * 4,
        out_specs=(ANY,) * 4,
        scratch_shapes=[
            pltpu.SemaphoreType.DMA((2, n)),
            pltpu.SemaphoreType.DMA((2, 3)),
            pltpu.SemaphoreType.DMA((4,)),
        ],
        compiler_params=pltpu.CompilerParams(collective_id=0, has_side_effects=True),
    )(own, queries, keys, values)
    meta = meta[:, 0, :3].reshape(-1)
    part = pltpu.VMEM((BLOCK, q_width + HEAD), bf)
    block = pltpu.VMEM((BLOCK, q_width), bf)
    dma = pltpu.SemaphoreType.DMA
    return pl.pallas_call(
        functools.partial(serve_kernel, n, reach),
        out_shape=shape(queries.shape, bf),
        in_specs=[SMEM, VMEM, VMEM, VMEM],
        out_specs=VMEM,
        scratch_shapes=[
            [block] * 2,
            pltpu.VMEM(k.shape, bf),
            pltpu.VMEM(v.shape, bf),
            pltpu.VMEM((2 * rows, HEAD), bf),
            [block] * (2 * reach),
            [part] * (2 * reach),
            [part] * (2 * reach),
            [part] * 2,
            pltpu.VMEM((BLOCK, width), bf),
            pltpu.VMEM((BLOCK, width), bf),
            pltpu.VMEM((BLOCK, HEAD), bf),
            pltpu.VMEM((width // HEAD, 2 * BLOCK, 2 * HEAD), jnp.float32),
            pltpu.VMEM((BLOCK, q_width), bf),
            pltpu.VMEM((BLOCK, q_width), bf),
            pltpu.VMEM((BLOCK, q_width), bf),
            dma((2, reach, 2)),
            dma((2, reach, 2)),
            dma((2, 3)),
            dma((2,)),
        ],
        compiler_params=pltpu.CompilerParams(
            collective_id=1, has_side_effects=True, vmem_limit_bytes=48 * 1024 * 1024
        ),
    )(meta, q, k, v)


def solution(mesh):
    placed = (
        P(("groups", "seq"), None),
        P(("groups", "seq"), None),
        P(("groups", "seq"), None),
        P(("groups", "seq")),
        P(("groups", "seq"), None),
    )
    return jax.shard_map(
        body, mesh=mesh, in_specs=placed, out_specs=P(("groups", "seq"), None), check_vma=False
    )
```

```python
import functools
import math

import jax
import jax.numpy as jnp
from jax import lax
from jax.experimental import pallas as pl
from jax.experimental.pallas import tpu as pltpu
from jax.sharding import PartitionSpec as P

HEAD = 128
WINDOW = 4096
BLOCK = 256
CAP = 50.0
QUERY_SCALE = 144.0 ** (-0.5)
LOG2E = math.log2(math.e)
VMEM = pl.BlockSpec(memory_space=pltpu.VMEM)
ANY = pl.BlockSpec(memory_space=pl.ANY)
SMEM = pl.BlockSpec(memory_space=pltpu.SMEM)
MESH = pl.DeviceIdType.MESH


def removed_before(meta, shard):
    def add(s, total):
        return total + meta[3 * s + 2] - meta[3 * s + 1]

    return lax.fori_loop(0, shard, add, jnp.int32(0))


def tables(row, base, begin, length):
    lane = lax.broadcasted_iota(jnp.int32, row.shape, 1)
    order = (lane % (HEAD // 2)).astype(jnp.float32)
    freq = jnp.exp(order * (-2.0 * math.log(10000.0) / HEAD))
    place = row - base - jnp.clip(row - begin, 0, length)
    angle = place.astype(jnp.float32) * freq
    low = lane < HEAD // 2
    cosine, sine = jnp.cos(angle), jnp.sin(angle)
    cosine_swap = pltpu.roll(cosine, HEAD // 2, 1)
    sine_swap = pltpu.roll(sine, HEAD // 2, 1)
    return (
        (jnp.where(low, cosine, cosine_swap), jnp.where(low, -sine, sine_swap)),
        (jnp.where(low, cosine_swap, cosine), jnp.where(low, -sine_swap, sine)),
    )


def rotate(x, table):
    x = x.astype(jnp.float32)
    return x * table[0] + pltpu.roll(x, HEAD // 2, 1) * table[1]


def at_seq(device):
    return {"seq": device}


def greet(conditions_devices):
    barrier = pltpu.get_barrier_semaphore()
    count = jnp.int32(0)
    for condition, device in conditions_devices:

        @pl.when(condition)
        def _():
            pl.semaphore_signal(barrier, inc=1, device_id=at_seq(device), device_id_type=MESH)

        count = count + jnp.where(condition, 1, 0)
    pl.semaphore_wait(barrier, count)


def exchange_kernel(n, own, meta, meta_sems, local_sem):
    me = lax.axis_index("seq")
    barrier = pltpu.get_barrier_semaphore()

    @pl.loop(1, n)
    def _(i):
        target = lax.rem(me + i, n)
        pl.semaphore_signal(barrier, inc=1, device_id=at_seq(target), device_id_type=MESH)

    pl.semaphore_wait(barrier, n - 1)

    def meta_copy(i, owner, target):
        return pltpu.make_async_remote_copy(
            src_ref=own,
            dst_ref=meta.at[owner],
            send_sem=meta_sems.at[0, i],
            recv_sem=meta_sems.at[1, owner],
            device_id=at_seq(target),
            device_id_type=MESH,
        )

    @pl.loop(1, n)
    def _(i):
        meta_copy(i, me, lax.rem(me + i, n)).start()

    local = pltpu.make_async_copy(own, meta.at[me], local_sem)
    local.start()
    local.wait()

    @pl.loop(1, n)
    def _(i):
        meta_copy(i, me, lax.rem(me + i, n)).wait_send()
        sender = lax.rem(me + n - i, n)
        meta_copy(i, sender, sender).wait_recv()


def rope_q(meta, shard, raw_rows, source, out):
    half = BLOCK // 2
    block = jnp.maximum(meta[3 * shard], 0)
    begin = meta[3 * shard + 1]
    length = meta[3 * shard + 2] - begin
    base = removed_before(meta, shard)
    raw0 = shard * raw_rows + block * BLOCK
    tile = 32

    @pl.loop(0, half // tile)
    def _(step):
        at = step * tile
        row = lax.broadcasted_iota(jnp.int32, (tile, HEAD), 0) + raw0 + at
        lane = lax.broadcasted_iota(jnp.int32, (tile, HEAD), 1)
        row = row + jnp.where(lane < HEAD // 2, 0, half)
        both = tables(row, base, begin, length)
        for part in range(2):
            here = pl.ds(pl.multiple_of(at + part * half, tile), tile)
            for h in range(out.shape[1] // HEAD):
                cols = pl.ds(h * HEAD, HEAD)
                x = rotate(source[here, cols], both[part]) * QUERY_SCALE
                out[here, cols] = x.astype(jnp.bfloat16)


def prepare(meta, shard, slot, k_ref, v_ref, k_out, v_out, live_out):
    rows = k_ref.shape[0]
    half = rows // 2
    begin = meta[3 * shard + 1]
    finish = meta[3 * shard + 2]
    base = removed_before(meta, shard)
    raw0 = shard * rows
    tile = 32

    @pl.loop(0, half // tile)
    def _(step):
        at = step * tile
        iota = lax.broadcasted_iota(jnp.int32, (tile, HEAD), 0)
        lane = lax.broadcasted_iota(jnp.int32, (tile, HEAD), 1)
        row = iota + raw0 + at + jnp.where(lane < HEAD // 2, 0, half)
        both = tables(row, base, begin, finish - begin)
        for part in range(2):
            src = at + part * half
            here = pl.ds(pl.multiple_of(src, tile), tile)
            place = pl.ds(pl.multiple_of(slot * rows + src, tile), tile)
            raw = iota + raw0 + src
            live = jnp.where((raw >= begin) & (raw < finish), 0.0, 1.0)
            live_out[place, :] = live.astype(jnp.bfloat16)
            for h in range(k_out.shape[1] // HEAD):
                cols = pl.ds(h * HEAD, HEAD)
                x = rotate(k_ref[here, cols], both[part])
                k_out[place, cols] = x.astype(jnp.bfloat16)
                y = v_ref[here, cols].astype(jnp.float32) * live
                v_out[place, cols] = y.astype(jnp.bfloat16)


def visit(q_ref, k_ref, v_ref, live_ref, acc, at, size, mask):
    kv_heads = k_ref.shape[1] // HEAD
    rows = pl.ds(at if isinstance(at, int) else pl.multiple_of(at, BLOCK), size)

    def scores(h):
        q = jnp.concatenate(
            [q_ref[:, pl.ds((2 * h + g) * HEAD, HEAD)] for g in range(2)], axis=0
        )
        k = k_ref[rows, pl.ds(h * HEAD, HEAD)]
        return lax.dot_general(
            q, k, (((1,), (1,)), ((), ())), preferred_element_type=jnp.float32
        )

    s = scores(0)
    for h in range(kv_heads):
        ahead = scores(h + 1) if h + 1 < kv_heads else None
        weight = jnp.exp2(jnp.tanh(s * (1.0 / CAP)) * (CAP * LOG2E))
        if mask is not None:
            weight = jnp.where(mask, weight, 0.0)
        v = jnp.concatenate([v_ref[rows, pl.ds(h * HEAD, HEAD)], live_ref[rows, :]], axis=1)
        acc[h] += jnp.dot(weight.astype(jnp.bfloat16), v, preferred_element_type=jnp.float32)
        s = ahead


def allowed(meta, n, shard_q, shard_k, raw_rows, at_k, size):
    shard_q = jnp.clip(shard_q, 0, n - 1)
    shard_k = jnp.clip(shard_k, 0, n - 1)
    column = lax.broadcasted_iota(jnp.int32, (2 * BLOCK, 1), 0)
    raw_q = shard_q * raw_rows + jnp.maximum(meta[3 * shard_q], 0) * BLOCK
    q = raw_q + jnp.where(column < BLOCK, column, column - BLOCK)
    k = shard_k * raw_rows + at_k + lax.broadcasted_iota(jnp.int32, (1, size), 1)
    begin_q, end_q = meta[3 * shard_q + 1], meta[3 * shard_q + 2]
    begin_k, end_k = meta[3 * shard_k + 1], meta[3 * shard_k + 2]
    between = removed_before(meta, shard_q) - removed_before(meta, shard_k)
    q_place = q - between - jnp.clip(q - begin_q, 0, end_q - begin_q)
    k_place = k - jnp.clip(k - begin_k, 0, end_k - begin_k)
    return (k <= q) & (q_place - k_place < WINDOW)


def pack(acc, out):
    kv_heads = acc.shape[0]
    lane = lax.broadcasted_iota(jnp.int32, (BLOCK, HEAD), 1)
    packed = jnp.zeros((BLOCK, HEAD), jnp.float32)
    for h in range(kv_heads):
        for part in range(2):
            head = 2 * h + part
            mine = pl.ds(part * BLOCK, BLOCK)
            out[:, pl.ds(head * HEAD, HEAD)] = acc[h, mine, pl.ds(0, HEAD)].astype(jnp.bfloat16)
            total = acc[h, mine, pl.ds(HEAD, HEAD)]
            coarse = total.astype(jnp.bfloat16).astype(jnp.float32)
            packed = jnp.where(lane == head, coarse, packed)
            packed = jnp.where(lane == head + 2 * kv_heads, total - coarse, packed)
    out[:, pl.ds(2 * kv_heads * HEAD, HEAD)] = packed.astype(jnp.bfloat16)


def finish(meta, shard, raw_rows, parts, out):
    heads = out.shape[1] // HEAD
    block = meta[3 * shard]
    begin, end = meta[3 * shard + 1], meta[3 * shard + 2]
    raw0 = shard * raw_rows + jnp.maximum(block, 0) * BLOCK
    tile = 64

    @pl.loop(0, BLOCK // tile)
    def _(step):
        here = pl.ds(pl.multiple_of(step * tile, tile), tile)
        raw = raw0 + step * tile + lax.broadcasted_iota(jnp.int32, (tile, HEAD), 0)
        keep = ((raw < begin) | (raw >= end)) & (block >= 0)
        totals = jnp.zeros((tile, HEAD), jnp.float32)
        for part in parts:
            totals += part[here, pl.ds(heads * HEAD, HEAD)].astype(jnp.float32)
        for h in range(heads):
            cols = pl.ds(h * HEAD, HEAD)
            total = totals[:, h : h + 1] + totals[:, heads + h : heads + h + 1]
            total = jnp.broadcast_to(jnp.where(total > 0, total, 1.0), (tile, HEAD))
            value = jnp.zeros((tile, HEAD), jnp.float32)
            for part in parts:
                value += part[here, cols].astype(jnp.float32)
            out[here, cols] = jnp.where(keep, value / total, 0.0).astype(jnp.bfloat16)


def serve_kernel(
    n, reach, meta, q_mine, q_other, k_mine, k_other, v_mine, v_other, out,
    q, k, v, live, q_in, part_out, part_in, own, tail_k, tail_v, tail_live, acc, done, give_away, got,
    q_sems, part_sems, tail_sems, done_sems,
):
    me = lax.axis_index("seq")
    core = lax.rem(me, 2)
    chip = lax.div(me, 2)
    chips = n // 2
    peer = me + 1 - 2 * core
    rows = k.shape[0] // 2
    per = rows // BLOCK
    far = reach + 1
    wide = 2 * BLOCK
    first = 2 * chip
    greet(
        [(me >= 0, peer)]
        + [(chip >= d, me - 2 * d) for d in range(1, far + 1)]
        + [(chip + d < chips, me + 2 * d) for d in range(1, far + 1)]
    )

    def q_copy(d, slot):
        return pltpu.make_async_remote_copy(
            src_ref=q[slot],
            dst_ref=q_in[2 * d - 2 + slot],
            send_sem=q_sems.at[0, d - 1, slot],
            recv_sem=q_sems.at[1, d - 1, slot],
            device_id=at_seq(jnp.maximum(me - 2 * d, core)),
            device_id_type=MESH,
        )

    def part_copy(d, slot):
        return pltpu.make_async_remote_copy(
            src_ref=part_out[2 * d - 2 + slot],
            dst_ref=part_in[2 * d - 2 + slot],
            send_sem=part_sems.at[0, d - 1, slot],
            recv_sem=part_sems.at[1, d - 1, slot],
            device_id=at_seq(jnp.minimum(me + 2 * d, n - 2 + core)),
            device_id_type=MESH,
        )

    last = pl.ds(2 * rows - BLOCK, BLOCK)
    tails = [
        pltpu.make_async_remote_copy(
            src_ref=source.at[last, :],
            dst_ref=target,
            send_sem=tail_sems.at[0, i],
            recv_sem=tail_sems.at[1, i],
            device_id=at_seq(jnp.minimum(me + 2 * far, n - 2 + core)),
            device_id_type=MESH,
        )
        for i, (source, target) in enumerate(((k, tail_k), (v, tail_v), (live, tail_live)))
    ]

    def forward(slot):
        return pltpu.make_async_remote_copy(
            src_ref=q_in[2 + slot],
            dst_ref=q_in[slot],
            send_sem=q_sems.at[0, 0, slot],
            recv_sem=q_sems.at[1, 0, slot],
            device_id=at_seq(jnp.minimum(me + 2, n - 2 + core)),
            device_id_type=MESH,
        )

    odd = lax.rem(chip, 2) == 1
    passes_on = jnp.logical_not(odd) & (chip + 2 < chips)

    def pass_on(slot):
        @pl.when(passes_on)
        def _():
            q_copy(2, slot).wait_recv()
            forward(slot).start()

    for slot in range(2):
        for side in range(2):

            @pl.when(core == side)
            def _():
                source = q_mine if side == slot else q_other
                rope_q(meta, first + slot, rows, source, q[slot])

    for slot in range(2):
        for d in range(reach, 0, -1):

            @pl.when((chip >= d) & odd if d == 1 else chip >= d)
            def _():
                q_copy(d, slot).start()

    for d in range(1, reach + 1):

        @pl.when(chip < d)
        def _():
            for ref in part_in[2 * d - 2 : 2 * d]:
                ref[...] = jnp.zeros_like(ref)

    prepare(meta, me, core, k_mine, v_mine, k, v, live)
    prepare(meta, peer, 1 - core, k_other, v_other, k, v, live)
    pass_on(0)

    @pl.when(chip + far < chips)
    def _():
        for copy in tails:
            copy.start()

    def masked(source, shard_q, j, size):
        shard_k = first + lax.div(j, per)
        mask = allowed(meta, n, shard_q, shard_k, rows, lax.rem(j, per) * BLOCK, size)
        visit(source, k, v, live, acc, j * BLOCK, size, mask)

    def plain(source, j):
        visit(source, k, v, live, acc, j * BLOCK, wide, None)

    def own_part(slot):
        acc[...] = jnp.zeros_like(acc)
        if slot == 1:

            @pl.loop(0, per // 2)
            def _(i):
                plain(q[slot], 2 * i)

        @pl.loop(0, per // 2)
        def _(i):
            masked(q[slot], first + slot, slot * per + 2 * i, wide)

    own_part(1)
    pack(acc, own[1])
    pass_on(1)

    for d in range(reach, 0, -1):

        @pl.when(chip + d < chips)
        def _():
            for slot in range(2):
                source = q_in[2 * d - 2 + slot]
                if d == 2:

                    @pl.when(jnp.logical_not(passes_on))
                    def _():
                        q_copy(d, slot).wait_recv()

                else:
                    q_copy(d, slot).wait_recv()
                acc[...] = jnp.zeros_like(acc)
                if d < reach:

                    @pl.loop(0, per)
                    def _(i):
                        plain(source, 2 * i)

                else:
                    shard_q = first + 2 * d + slot

                    @pl.loop(0, per // 2)
                    def _(i):
                        masked(source, shard_q, slot * per + 2 * i, wide)

                    if slot == 0:

                        @pl.loop(0, per // 2)
                        def _(i):
                            plain(source, per + 2 * i)

                    else:
                        masked(source, shard_q, jnp.int32(per - 1), BLOCK)

                pack(acc, part_out[2 * d - 2 + slot])
                part_copy(d, slot).start()

    own_part(0)

    @pl.when(chip >= far)
    def _():
        for copy in tails:
            copy.wait_recv()
        mask = allowed(meta, n, first, first - 2 * far + 1, rows, rows - BLOCK, BLOCK)
        visit(q[0], tail_k, tail_v, tail_live, acc, 0, BLOCK, mask)

    pack(acc, own[0])
    for d in range(1, reach + 1):

        @pl.when(chip >= d)
        def _():
            for slot in range(2):
                part_copy(d, slot).wait_recv()

    def final(slot, out):
        finish(meta, first + slot, rows, [own[slot]] + list(part_in[slot::2]), out)

    for slot in range(2):

        @pl.when(core == slot)
        def _():
            final(1 - slot, give_away)

    give = pltpu.make_async_remote_copy(
        src_ref=give_away,
        dst_ref=got,
        send_sem=done_sems.at[0],
        recv_sem=done_sems.at[1],
        device_id=at_seq(peer),
        device_id_type=MESH,
    )
    give.start()
    for slot in range(2):

        @pl.when(core == slot)
        def _():
            final(slot, done)

    width = done.shape[1]
    out[:, pl.ds(pl.multiple_of(core * width, HEAD), width)] = done[...]
    give.wait()
    out[:, pl.ds(pl.multiple_of((1 - core) * width, HEAD), width)] = got[...]

    for d in range(1, reach + 1):

        @pl.when((chip >= d) & odd if d == 1 else chip >= d)
        def _():
            for slot in range(2):
                q_copy(d, slot).wait_send()

        @pl.when(chip + d < chips)
        def _():
            for slot in range(2):
                part_copy(d, slot).wait_send()

    @pl.when(passes_on)
    def _():
        for slot in range(2):
            forward(slot).wait_send()

    @pl.when(chip + far < chips)
    def _():
        for copy in tails:
            copy.wait_send()


def body(queries, keys, values, dirty, spans):
    n = lax.axis_size("seq")
    bf = jnp.bfloat16
    shape = jax.ShapeDtypeStruct
    rows, width = keys.shape[0], keys.shape[1] // 2
    q_width = queries.shape[1] // 2
    reach = WINDOW // (2 * rows)
    core = lax.axis_index("seq") % 2
    pairs = [(i, i ^ 1) for i in range(n)]
    halves = []
    for array in (queries, keys, values):
        half = array.shape[1] // 2
        low, high = array[:, :half], array[:, half:]
        mine = jnp.where(core == 0, low, high)
        halves += [mine, lax.ppermute(jnp.where(core == 0, high, low), "seq", pairs)]
    own = jnp.concatenate([dirty[:, None], spans], axis=1)
    own = jnp.pad(own, ((0, 7), (0, HEAD - 3)))
    meta = pl.pallas_call(
        functools.partial(exchange_kernel, n),
        out_shape=shape((n, 8, HEAD), jnp.int32),
        in_specs=[VMEM],
        out_specs=VMEM,
        scratch_shapes=[pltpu.SemaphoreType.DMA((2, n)), pltpu.SemaphoreType.DMA],
        compiler_params=pltpu.CompilerParams(collective_id=0, has_side_effects=True),
    )(own)
    meta = meta[:, 0, :3].reshape(-1)
    part = pltpu.VMEM((BLOCK, q_width + HEAD), bf)
    block = pltpu.VMEM((BLOCK, q_width), bf)
    dma = pltpu.SemaphoreType.DMA
    return pl.pallas_call(
        functools.partial(serve_kernel, n, reach),
        out_shape=shape(queries.shape, bf),
        in_specs=[SMEM] + [VMEM] * 6,
        out_specs=VMEM,
        scratch_shapes=[
            [block] * 2,
            pltpu.VMEM((2 * rows, width), bf),
            pltpu.VMEM((2 * rows, width), bf),
            pltpu.VMEM((2 * rows, HEAD), bf),
            [block] * (2 * reach),
            [part] * (2 * reach),
            [part] * (2 * reach),
            [part] * 2,
            pltpu.VMEM((BLOCK, width), bf),
            pltpu.VMEM((BLOCK, width), bf),
            pltpu.VMEM((BLOCK, HEAD), bf),
            pltpu.VMEM((width // HEAD, 2 * BLOCK, 2 * HEAD), jnp.float32),
            pltpu.VMEM((BLOCK, q_width), bf),
            pltpu.VMEM((BLOCK, q_width), bf),
            pltpu.VMEM((BLOCK, q_width), bf),
            dma((2, reach, 2)),
            dma((2, reach, 2)),
            dma((2, 3)),
            dma((2,)),
        ],
        compiler_params=pltpu.CompilerParams(
            collective_id=1, has_side_effects=True, vmem_limit_bytes=48 * 1024 * 1024
        ),
    )(meta, *halves)


def solution(mesh):
    placed = (
        P(("groups", "seq"), None),
        P(("groups", "seq"), None),
        P(("groups", "seq"), None),
        P(("groups", "seq")),
        P(("groups", "seq"), None),
    )
    return jax.shard_map(
        body, mesh=mesh, in_specs=placed, out_specs=P(("groups", "seq"), None), check_vma=False
    )
```

```python
import functools
import math

import jax
import jax.numpy as jnp
from jax import lax
from jax.experimental import pallas as pl
from jax.experimental.pallas import tpu as pltpu
from jax.sharding import PartitionSpec as P

HEAD = 128
WINDOW = 4096
BLOCK = 256
TILE = 32
CAP = 50.0
QUERY_SCALE = 144.0 ** (-0.5)
LOG2E = math.log2(math.e)
VMEM = pl.BlockSpec(memory_space=pltpu.VMEM)
ANY = pl.BlockSpec(memory_space=pl.ANY)
SMEM = pl.BlockSpec(memory_space=pltpu.SMEM)
MESH = pl.DeviceIdType.MESH


def removed_before(meta, shard):
    def add(s, total):
        return total + meta[3 * s + 2] - meta[3 * s + 1]

    return lax.fori_loop(0, shard, add, jnp.int32(0))


def frequency(shape):
    lane = lax.broadcasted_iota(jnp.int32, shape, 1)
    order = (lane % (HEAD // 2)).astype(jnp.float32)
    return jnp.exp(order * (-2.0 * math.log(10000.0) / HEAD))


def row_tables():
    row = lax.broadcasted_iota(jnp.int32, (TILE, HEAD), 0)
    angle = row.astype(jnp.float32) * frequency(row.shape)
    return jnp.cos(angle), jnp.sin(angle)


def tables(start, base, begin, length, small):
    which = lax.broadcasted_iota(jnp.int32, (8, HEAD), 0)
    place = start - base + (which // 2) * TILE - jnp.where(which % 2 == 1, length, 0)
    angle = place.astype(jnp.float32) * frequency(which.shape)
    cosine, sine = jnp.cos(angle), jnp.sin(angle)
    row = lax.broadcasted_iota(jnp.int32, (TILE, HEAD), 0)
    low = lax.broadcasted_iota(jnp.int32, (TILE, HEAD), 1) < HEAD // 2
    result = []
    for t in range(4):
        after = row + (start + t * TILE) >= begin
        c = jnp.where(after, cosine[2 * t + 1 : 2 * t + 2], cosine[2 * t : 2 * t + 1])
        s = jnp.where(after, sine[2 * t + 1 : 2 * t + 2], sine[2 * t : 2 * t + 1])
        turned = s * small[0] + c * small[1]
        result.append((c * small[0] - s * small[1], jnp.where(low, -turned, turned)))
    return result


def rotate(x, table):
    x = x.astype(jnp.float32)
    return x * table[0] + pltpu.roll(x, HEAD // 2, 1) * table[1]


def at_seq(device):
    return {"seq": device}


def greet(conditions_devices):
    barrier = pltpu.get_barrier_semaphore()
    count = jnp.int32(0)
    for condition, device in conditions_devices:

        @pl.when(condition)
        def _():
            pl.semaphore_signal(barrier, inc=1, device_id=at_seq(device), device_id_type=MESH)

        count = count + jnp.where(condition, 1, 0)
    pl.semaphore_wait(barrier, count)


def exchange_kernel(n, own, meta, meta_sems, local_sem):
    me = lax.axis_index("seq")
    barrier = pltpu.get_barrier_semaphore()

    @pl.loop(1, n)
    def _(i):
        target = lax.rem(me + i, n)
        pl.semaphore_signal(barrier, inc=1, device_id=at_seq(target), device_id_type=MESH)

    pl.semaphore_wait(barrier, n - 1)

    def meta_copy(i, owner, target):
        return pltpu.make_async_remote_copy(
            src_ref=own,
            dst_ref=meta.at[owner],
            send_sem=meta_sems.at[0, i],
            recv_sem=meta_sems.at[1, owner],
            device_id=at_seq(target),
            device_id_type=MESH,
        )

    @pl.loop(1, n)
    def _(i):
        meta_copy(i, me, lax.rem(me + i, n)).start()

    local = pltpu.make_async_copy(own, meta.at[me], local_sem)
    local.start()
    local.wait()

    @pl.loop(1, n)
    def _(i):
        meta_copy(i, me, lax.rem(me + i, n)).wait_send()
        sender = lax.rem(me + n - i, n)
        meta_copy(i, sender, sender).wait_recv()


def rope_q(meta, shard, raw_rows, source, out, small):
    block = jnp.maximum(meta[3 * shard], 0)
    begin = meta[3 * shard + 1]
    length = meta[3 * shard + 2] - begin
    base = removed_before(meta, shard)
    raw0 = shard * raw_rows + block * BLOCK

    @pl.loop(0, BLOCK // (4 * TILE))
    def _(step):
        at = step * (4 * TILE)
        for part, table in enumerate(tables(raw0 + at, base, begin, length, small)):
            here = pl.ds(pl.multiple_of(at + part * TILE, TILE), TILE)
            for h in range(out.shape[1] // HEAD):
                cols = pl.ds(h * HEAD, HEAD)
                x = rotate(source[here, cols], table) * QUERY_SCALE
                out[here, cols] = x.astype(jnp.bfloat16)


def prepare(meta, shard, slot, k_ref, v_ref, k_out, v_out, live_out, small):
    rows = k_ref.shape[0]
    begin = meta[3 * shard + 1]
    finish = meta[3 * shard + 2]
    base = removed_before(meta, shard)
    raw0 = shard * rows

    @pl.loop(0, rows // (4 * TILE))
    def _(step):
        at = step * (4 * TILE)
        iota = lax.broadcasted_iota(jnp.int32, (TILE, HEAD), 0)
        turns = tables(raw0 + at, base, begin, finish - begin, small)
        for part, table in enumerate(turns):
            src = at + part * TILE
            here = pl.ds(pl.multiple_of(src, TILE), TILE)
            place = pl.ds(pl.multiple_of(slot * rows + src, TILE), TILE)
            raw = iota + raw0 + src
            live = jnp.where((raw >= begin) & (raw < finish), 0.0, 1.0)
            live_out[place, :] = live.astype(jnp.bfloat16)
            for h in range(k_out.shape[1] // HEAD):
                cols = pl.ds(h * HEAD, HEAD)
                k_out[place, cols] = rotate(k_ref[here, cols], table).astype(jnp.bfloat16)
                y = v_ref[here, cols].astype(jnp.float32) * live
                v_out[place, cols] = y.astype(jnp.bfloat16)


def visit(q_ref, k_ref, v_ref, live_ref, acc, at, size, mask):
    kv_heads = k_ref.shape[1] // HEAD
    rows = pl.ds(at if isinstance(at, int) else pl.multiple_of(at, BLOCK), size)

    def scores(h):
        q = jnp.concatenate(
            [q_ref[:, pl.ds((2 * h + g) * HEAD, HEAD)] for g in range(2)], axis=0
        )
        k = k_ref[rows, pl.ds(h * HEAD, HEAD)]
        return lax.dot_general(
            q, k, (((1,), (1,)), ((), ())), preferred_element_type=jnp.float32
        )

    s = scores(0)
    for h in range(kv_heads):
        ahead = scores(h + 1) if h + 1 < kv_heads else None
        weight = jnp.exp2(jnp.tanh(s * (1.0 / CAP)) * (CAP * LOG2E))
        if mask is not None:
            weight = jnp.where(mask, weight, 0.0)
        v = jnp.concatenate([v_ref[rows, pl.ds(h * HEAD, HEAD)], live_ref[rows, :]], axis=1)
        acc[h] += jnp.dot(weight.astype(jnp.bfloat16), v, preferred_element_type=jnp.float32)
        s = ahead


def allowed(meta, n, shard_q, shard_k, raw_rows, at_k, size):
    shard_q = jnp.clip(shard_q, 0, n - 1)
    shard_k = jnp.clip(shard_k, 0, n - 1)
    column = lax.broadcasted_iota(jnp.int32, (2 * BLOCK, 1), 0)
    raw_q = shard_q * raw_rows + jnp.maximum(meta[3 * shard_q], 0) * BLOCK
    q = raw_q + jnp.where(column < BLOCK, column, column - BLOCK)
    k = shard_k * raw_rows + at_k + lax.broadcasted_iota(jnp.int32, (1, size), 1)
    begin_q, end_q = meta[3 * shard_q + 1], meta[3 * shard_q + 2]
    begin_k, end_k = meta[3 * shard_k + 1], meta[3 * shard_k + 2]
    between = removed_before(meta, shard_q) - removed_before(meta, shard_k)
    q_place = q - between - jnp.clip(q - begin_q, 0, end_q - begin_q)
    k_place = k - jnp.clip(k - begin_k, 0, end_k - begin_k)
    return (k <= q) & (q_place - k_place < WINDOW)


def pack(acc, out):
    kv_heads = acc.shape[0]
    lane = lax.broadcasted_iota(jnp.int32, (BLOCK, HEAD), 1)
    packed = jnp.zeros((BLOCK, HEAD), jnp.float32)
    for h in range(kv_heads):
        for part in range(2):
            head = 2 * h + part
            mine = pl.ds(part * BLOCK, BLOCK)
            out[:, pl.ds(head * HEAD, HEAD)] = acc[h, mine, pl.ds(0, HEAD)].astype(jnp.bfloat16)
            total = acc[h, mine, pl.ds(HEAD, HEAD)]
            coarse = total.astype(jnp.bfloat16).astype(jnp.float32)
            packed = jnp.where(lane == head, coarse, packed)
            packed = jnp.where(lane == head + 2 * kv_heads, total - coarse, packed)
    out[:, pl.ds(2 * kv_heads * HEAD, HEAD)] = packed.astype(jnp.bfloat16)


def finish(meta, shard, raw_rows, parts, out):
    heads = out.shape[1] // HEAD
    block = meta[3 * shard]
    begin, end = meta[3 * shard + 1], meta[3 * shard + 2]
    raw0 = shard * raw_rows + jnp.maximum(block, 0) * BLOCK
    tile = 64

    @pl.loop(0, BLOCK // tile)
    def _(step):
        here = pl.ds(pl.multiple_of(step * tile, tile), tile)
        raw = raw0 + step * tile + lax.broadcasted_iota(jnp.int32, (tile, HEAD), 0)
        keep = ((raw < begin) | (raw >= end)) & (block >= 0)
        totals = jnp.zeros((tile, HEAD), jnp.float32)
        for part in parts:
            totals += part[here, pl.ds(heads * HEAD, HEAD)].astype(jnp.float32)
        for h in range(heads):
            cols = pl.ds(h * HEAD, HEAD)
            total = totals[:, h : h + 1] + totals[:, heads + h : heads + h + 1]
            total = jnp.broadcast_to(jnp.where(total > 0, total, 1.0), (tile, HEAD))
            value = jnp.zeros((tile, HEAD), jnp.float32)
            for part in parts:
                value += part[here, cols].astype(jnp.float32)
            out[here, cols] = jnp.where(keep, value / total, 0.0).astype(jnp.bfloat16)


def serve_kernel(
    n, reach, meta, q_mine, q_other, k_mine, k_other, v_mine, v_other, out,
    q, k, v, live, q_in, part_out, part_in, own, tail_k, tail_v, tail_live, acc, done, give_away, got,
    q_sems, part_sems, tail_sems, done_sems,
):
    me = lax.axis_index("seq")
    core = lax.rem(me, 2)
    chip = lax.div(me, 2)
    chips = n // 2
    peer = me + 1 - 2 * core
    rows = k.shape[0] // 2
    per = rows // BLOCK
    far = reach + 1
    wide = 2 * BLOCK
    first = 2 * chip
    greet(
        [(me >= 0, peer)]
        + [(chip >= d, me - 2 * d) for d in range(1, far + 1)]
        + [(chip + d < chips, me + 2 * d) for d in range(1, far + 1)]
    )

    def q_copy(d, slot):
        return pltpu.make_async_remote_copy(
            src_ref=q[slot],
            dst_ref=q_in[2 * d - 2 + slot],
            send_sem=q_sems.at[0, d - 1, slot],
            recv_sem=q_sems.at[1, d - 1, slot],
            device_id=at_seq(jnp.maximum(me - 2 * d, core)),
            device_id_type=MESH,
        )

    def part_copy(d, slot):
        return pltpu.make_async_remote_copy(
            src_ref=part_out[2 * d - 2 + slot],
            dst_ref=part_in[2 * d - 2 + slot],
            send_sem=part_sems.at[0, d - 1, slot],
            recv_sem=part_sems.at[1, d - 1, slot],
            device_id=at_seq(jnp.minimum(me + 2 * d, n - 2 + core)),
            device_id_type=MESH,
        )

    last = pl.ds(2 * rows - BLOCK, BLOCK)
    tails = [
        pltpu.make_async_remote_copy(
            src_ref=source.at[last, :],
            dst_ref=target,
            send_sem=tail_sems.at[0, i],
            recv_sem=tail_sems.at[1, i],
            device_id=at_seq(jnp.minimum(me + 2 * far, n - 2 + core)),
            device_id_type=MESH,
        )
        for i, (source, target) in enumerate(((k, tail_k), (v, tail_v), (live, tail_live)))
    ]

    def forward(slot):
        return pltpu.make_async_remote_copy(
            src_ref=q_in[2 + slot],
            dst_ref=q_in[slot],
            send_sem=q_sems.at[0, 0, slot],
            recv_sem=q_sems.at[1, 0, slot],
            device_id=at_seq(jnp.minimum(me + 2, n - 2 + core)),
            device_id_type=MESH,
        )

    odd = lax.rem(chip, 2) == 1
    passes_on = jnp.logical_not(odd) & (chip + 2 < chips)

    def pass_on(slot):
        @pl.when(passes_on)
        def _():
            q_copy(2, slot).wait_recv()
            forward(slot).start()

    small = row_tables()
    for slot in range(2):
        for side in range(2):

            @pl.when(core == side)
            def _():
                source = q_mine if side == slot else q_other
                rope_q(meta, first + slot, rows, source, q[slot], small)

    for slot in range(2):
        for d in range(reach, 0, -1):

            @pl.when((chip >= d) & odd if d == 1 else chip >= d)
            def _():
                q_copy(d, slot).start()

    for d in range(1, reach + 1):

        @pl.when(chip < d)
        def _():
            for ref in part_in[2 * d - 2 : 2 * d]:
                ref[...] = jnp.zeros_like(ref)

    prepare(meta, me, core, k_mine, v_mine, k, v, live, small)
    prepare(meta, peer, 1 - core, k_other, v_other, k, v, live, small)
    pass_on(0)

    @pl.when(chip + far < chips)
    def _():
        for copy in tails:
            copy.start()

    def masked(source, shard_q, j, size):
        shard_k = first + lax.div(j, per)
        mask = allowed(meta, n, shard_q, shard_k, rows, lax.rem(j, per) * BLOCK, size)
        visit(source, k, v, live, acc, j * BLOCK, size, mask)

    def plain(source, j):
        visit(source, k, v, live, acc, j * BLOCK, wide, None)

    def own_part(slot):
        acc[...] = jnp.zeros_like(acc)
        if slot == 1:

            @pl.loop(0, per // 2)
            def _(i):
                plain(q[slot], 2 * i)

        @pl.loop(0, per // 2)
        def _(i):
            masked(q[slot], first + slot, slot * per + 2 * i, wide)

    own_part(1)
    pack(acc, own[1])
    pass_on(1)

    for d in range(reach, 0, -1):

        @pl.when(chip + d < chips)
        def _():
            for slot in range(2):
                source = q_in[2 * d - 2 + slot]
                if d == 2:

                    @pl.when(jnp.logical_not(passes_on))
                    def _():
                        q_copy(d, slot).wait_recv()

                else:
                    q_copy(d, slot).wait_recv()
                acc[...] = jnp.zeros_like(acc)
                if d < reach:

                    @pl.loop(0, per)
                    def _(i):
                        plain(source, 2 * i)

                else:
                    shard_q = first + 2 * d + slot

                    @pl.loop(0, per // 2)
                    def _(i):
                        masked(source, shard_q, slot * per + 2 * i, wide)

                    if slot == 0:

                        @pl.loop(0, per // 2)
                        def _(i):
                            plain(source, per + 2 * i)

                    else:
                        masked(source, shard_q, jnp.int32(per - 1), BLOCK)

                pack(acc, part_out[2 * d - 2 + slot])
                part_copy(d, slot).start()

    own_part(0)

    @pl.when(chip >= far)
    def _():
        for copy in tails:
            copy.wait_recv()
        mask = allowed(meta, n, first, first - 2 * far + 1, rows, rows - BLOCK, BLOCK)
        visit(q[0], tail_k, tail_v, tail_live, acc, 0, BLOCK, mask)

    pack(acc, own[0])
    for d in range(1, reach + 1):

        @pl.when(chip >= d)
        def _():
            for slot in range(2):
                part_copy(d, slot).wait_recv()

    def final(slot, out):
        finish(meta, first + slot, rows, [own[slot]] + list(part_in[slot::2]), out)

    for slot in range(2):

        @pl.when(core == slot)
        def _():
            final(1 - slot, give_away)

    give = pltpu.make_async_remote_copy(
        src_ref=give_away,
        dst_ref=got,
        send_sem=done_sems.at[0],
        recv_sem=done_sems.at[1],
        device_id=at_seq(peer),
        device_id_type=MESH,
    )
    give.start()
    for slot in range(2):

        @pl.when(core == slot)
        def _():
            final(slot, done)

    width = done.shape[1]
    out[:, pl.ds(pl.multiple_of(core * width, HEAD), width)] = done[...]
    give.wait()
    out[:, pl.ds(pl.multiple_of((1 - core) * width, HEAD), width)] = got[...]

    for d in range(1, reach + 1):

        @pl.when((chip >= d) & odd if d == 1 else chip >= d)
        def _():
            for slot in range(2):
                q_copy(d, slot).wait_send()

        @pl.when(chip + d < chips)
        def _():
            for slot in range(2):
                part_copy(d, slot).wait_send()

    @pl.when(passes_on)
    def _():
        for slot in range(2):
            forward(slot).wait_send()

    @pl.when(chip + far < chips)
    def _():
        for copy in tails:
            copy.wait_send()


def body(queries, keys, values, dirty, spans):
    n = lax.axis_size("seq")
    bf = jnp.bfloat16
    shape = jax.ShapeDtypeStruct
    rows, width = keys.shape[0], keys.shape[1] // 2
    q_width = queries.shape[1] // 2
    reach = WINDOW // (2 * rows)
    core = lax.axis_index("seq") % 2
    pairs = [(i, i ^ 1) for i in range(n)]
    halves = []
    for array in (queries, keys, values):
        half = array.shape[1] // 2
        low, high = array[:, :half], array[:, half:]
        mine = jnp.where(core == 0, low, high)
        halves += [mine, lax.ppermute(jnp.where(core == 0, high, low), "seq", pairs)]
    own = jnp.concatenate([dirty[:, None], spans], axis=1)
    own = jnp.pad(own, ((0, 7), (0, HEAD - 3)))
    meta = pl.pallas_call(
        functools.partial(exchange_kernel, n),
        out_shape=shape((n, 8, HEAD), jnp.int32),
        in_specs=[VMEM],
        out_specs=VMEM,
        scratch_shapes=[pltpu.SemaphoreType.DMA((2, n)), pltpu.SemaphoreType.DMA],
        compiler_params=pltpu.CompilerParams(collective_id=0, has_side_effects=True),
    )(own)
    meta = meta[:, 0, :3].reshape(-1)
    part = pltpu.VMEM((BLOCK, q_width + HEAD), bf)
    block = pltpu.VMEM((BLOCK, q_width), bf)
    dma = pltpu.SemaphoreType.DMA
    return pl.pallas_call(
        functools.partial(serve_kernel, n, reach),
        out_shape=shape(queries.shape, bf),
        in_specs=[SMEM] + [VMEM] * 6,
        out_specs=VMEM,
        scratch_shapes=[
            [block] * 2,
            pltpu.VMEM((2 * rows, width), bf),
            pltpu.VMEM((2 * rows, width), bf),
            pltpu.VMEM((2 * rows, HEAD), bf),
            [block] * (2 * reach),
            [part] * (2 * reach),
            [part] * (2 * reach),
            [part] * 2,
            pltpu.VMEM((BLOCK, width), bf),
            pltpu.VMEM((BLOCK, width), bf),
            pltpu.VMEM((BLOCK, HEAD), bf),
            pltpu.VMEM((width // HEAD, 2 * BLOCK, 2 * HEAD), jnp.float32),
            pltpu.VMEM((BLOCK, q_width), bf),
            pltpu.VMEM((BLOCK, q_width), bf),
            pltpu.VMEM((BLOCK, q_width), bf),
            dma((2, reach, 2)),
            dma((2, reach, 2)),
            dma((2, 3)),
            dma((2,)),
        ],
        compiler_params=pltpu.CompilerParams(
            collective_id=1, has_side_effects=True, vmem_limit_bytes=48 * 1024 * 1024
        ),
    )(meta, *halves)


def solution(mesh):
    placed = (
        P(("groups", "seq"), None),
        P(("groups", "seq"), None),
        P(("groups", "seq"), None),
        P(("groups", "seq")),
        P(("groups", "seq"), None),
    )
    return jax.shard_map(
        body, mesh=mesh, in_specs=placed, out_specs=P(("groups", "seq"), None), check_vma=False
    )
```
